32 devices in a mesh: parts: 2 (over y), slab: 4 (over z), section: 2 (over x), col: 2 (over core).
Axes of the slice: x: 2, y: 2, z: 4, core: 2. Of those that a mesh axis runs over, the one named last changes fastest.
Arguments:
- material_share: float32 [32, 256, 256], P(('parts', 'slab'), 'col', 'section'), parts along dimension 0, may hold values from 0.05 to 1
- stored_thermal_state: float32 [8, 16, 256, 256], P(('parts', 'section'), 'slab', 'col'), parts along dimension 0, may hold values from -6 to 6
- objective_slope: float32 [8, 16, 256, 256], P(('parts', 'section'), 'slab', 'col'), parts along dimension 0, may hold values from -6 to 6
- print_depths: int32 [8], P(('parts', 'section')), parts along dimension 0, may hold values from 1 to 16, as said below
- slice_to_deposit: int32 [32], P('parts'), parts along dimension 0, may hold values from 0 to 15, each once
Outputs:
- costate_temp: float32 [8, 16, 256, 256], P(('parts', 'section'), 'slab', 'col'), parts along dimension 0
- sensitivity: float32 [32, 256, 256], P(('parts', 'slab'), 'col', 'section'), parts along dimension 0
The draws below stay inside these ranges and needn't reach their ends.
There are 2 independent parts, one for each index of `parts`. The reference program is written for one: setup_inputs(seed, part) draws one part's arguments, and reference() takes and returns one part's arrays. A program takes and returns all parts, laid end to end along the dimension named above; each array names one. Nothing has to cross between parts.
Inputs may be any that keep to these rules, and one draw needn't show every extreme that they name: `print_depths`: the planes present at a section are those whose build layer is under its height; in every draw some section has all 16 layers and some section only one. `slice_to_deposit`: every layer number appears at exactly one plane.
All inputs are finite; a program needn't handle non-finite values.
Results may differ from the reference program's by a relative error of at most 0.0003.
Values sent between devices are 32-bit elements; how exact they have to be, the bound alone decides.
A program may use at most 64 MiB of HBM per device.

```python
import jax
import jax.numpy as jnp
from jax import lax

VOXELS_ACROSS = 256
SWEEPS = 6
SPAN_SLICES = 16
LINES_IN_SLICE = 256
PRINT_STEPS = 4


def draw_print_depths(key, part):
    key_draw, key_pick = jax.random.split(key)
    values = jax.random.randint(key_draw, (PRINT_STEPS,), 1, SPAN_SLICES + 1).astype(jnp.int32)
    shuffled = jax.random.permutation(key_pick, PRINT_STEPS)
    values = values.at[shuffled[0]].set(SPAN_SLICES)
    values = values.at[shuffled[1]].set(1)
    return values


def level_of(own_key, shape, pieces, low, top_value):
    loudness, own = 1.0, jax.random.fold_in(own_key, 6)
    for axis_at, blocks in pieces:
        steps = jnp.exp(jax.random.uniform(jax.random.fold_in(own, axis_at), (blocks,), jnp.float32, low / len(pieces), top_value / len(pieces)))
        loudness = loudness * jnp.repeat(steps, shape[axis_at] // blocks).reshape([-1 if axis == axis_at else 1 for axis in range(len(shape))])
    return loudness


def bell_draw(key, dims, deviation, reach, shards=(), kind=jnp.bfloat16):
    level = level_of(key, dims, shards, -0.22, 0.18) if shards else 1.0
    drawn = jax.random.normal(key, dims, jnp.float32) * deviation * level
    return jnp.minimum(jnp.maximum(drawn, -reach), reach).astype(kind)


def setup_inputs(seed: int = 0, part: int = 0) -> dict:
    keys = jax.random.split(jax.random.key(seed), 6)
    own_keys = jax.random.split(jax.random.fold_in(keys[5], part), 6)
    return {
        "material_share": jnp.clip(0.05 + 0.95 * jax.random.uniform(own_keys[0], (SPAN_SLICES, LINES_IN_SLICE, VOXELS_ACROSS), jnp.float32) ** level_of(own_keys[0], (SPAN_SLICES, LINES_IN_SLICE, VOXELS_ACROSS), ((0, 4), (1, 2), (2, 2)), -0.2, 0.2), 0.05, 1.0),
        "stored_thermal_state": bell_draw(own_keys[1], (PRINT_STEPS, SPAN_SLICES, LINES_IN_SLICE, VOXELS_ACROSS), 1.0, 6.0, ((0, 2), (1, 4), (2, 2)), jnp.float32),
        "objective_slope": bell_draw(own_keys[2], (PRINT_STEPS, SPAN_SLICES, LINES_IN_SLICE, VOXELS_ACROSS), 1.0, 6.0, ((0, 2), (1, 4), (2, 2)), jnp.float32),
        "print_depths": draw_print_depths(jax.random.fold_in(jax.random.fold_in(keys[5], part), 71), part),
        "slice_to_deposit": jax.random.permutation(own_keys[4], SPAN_SLICES).astype(jnp.int32),
    }


LOSS_RATE = 0.05
FLOOR_COND = 0.001
SIMP_POWER = 3.0
BOUND_LOW = 0.05
BOUND_HIGH = 2.0


def conduct(material_share):
    return FLOOR_COND + (1.0 - FLOOR_COND) * material_share ** 3


def face_weights(conduction, active):
    z_inner = 0.5 * active[1:] * active[:-1] * (conduction[1:] + conduction[:-1])
    y_inner = 0.5 * active[:, 1:] * active[:, :-1] * (conduction[:, 1:] + conduction[:, :-1])
    x_inner = 0.5 * active[:, :, 1:] * active[:, :, :-1] * (conduction[:, :, 1:] + conduction[:, :, :-1])
    z_face = jnp.pad(z_inner, ((1, 1), (0, 0), (0, 0)))
    y_face = jnp.pad(y_inner, ((0, 0), (1, 1), (0, 0)))
    x_face = jnp.pad(x_inner, ((0, 0), (0, 0), (1, 1)))
    diagonal = LOSS_RATE * active + (1.0 - active) + z_face[:-1] + z_face[1:] + y_face[:, :-1] + y_face[:, 1:] + x_face[:, :, :-1] + x_face[:, :, 1:]
    return z_face, y_face, x_face, diagonal


def operate(values_in, z_face, y_face, x_face, diagonal):
    padded = jnp.pad(values_in, 1)
    return (diagonal * values_in
            - z_face[:-1] * padded[:-2, 1:-1, 1:-1] - z_face[1:] * padded[2:, 1:-1, 1:-1]
            - y_face[:, :-1] * padded[1:-1, :-2, 1:-1] - y_face[:, 1:] * padded[1:-1, 2:, 1:-1]
            - x_face[:, :, :-1] * padded[1:-1, 1:-1, :-2] - x_face[:, :, 1:] * padded[1:-1, 1:-1, 2:])


def face_energy(costate_temp, saved_temp, active):
    z_term = 0.5 * active[1:] * active[:-1] * (costate_temp[1:] - costate_temp[:-1]) * (saved_temp[1:] - saved_temp[:-1])
    y_term = 0.5 * active[:, 1:] * active[:, :-1] * (costate_temp[:, 1:] - costate_temp[:, :-1]) * (saved_temp[:, 1:] - saved_temp[:, :-1])
    x_term = 0.5 * active[:, :, 1:] * active[:, :, :-1] * (costate_temp[:, :, 1:] - costate_temp[:, :, :-1]) * (saved_temp[:, :, 1:] - saved_temp[:, :, :-1])
    z_term = jnp.pad(z_term, ((1, 1), (0, 0), (0, 0)))
    y_term = jnp.pad(y_term, ((0, 0), (1, 1), (0, 0)))
    x_term = jnp.pad(x_term, ((0, 0), (0, 0), (1, 1)))
    return (z_term[:-1] + z_term[1:]) + (y_term[:, :-1] + y_term[:, 1:]) + (x_term[:, :, :-1] + x_term[:, :, 1:])


def reference(material_share, stored_thermal_state, objective_slope, print_depths, slice_to_deposit):
    conduction = conduct(material_share)
    center = 0.5 * (BOUND_HIGH + BOUND_LOW)
    half_width = 0.5 * (BOUND_HIGH - BOUND_LOW)
    cheb_ratio = center / half_width

    def lone_partial_print(section_item):
        saved_temp, section_grad, height = section_item
        active = jnp.broadcast_to((slice_to_deposit < height).astype(jnp.float32)[:, None, None], conduction.shape)
        z_face, y_face, x_face, diagonal = face_weights(conduction, active)
        source = active * section_grad
        update = source / diagonal / center
        adjoint_field = update
        factor = 1.0 / cheb_ratio
        for sweep_index in range(1, SWEEPS):
            residue = source - operate(adjoint_field, z_face, y_face, x_face, diagonal)
            factor_next = 1.0 / (2.0 * cheb_ratio - factor)
            update = factor_next * factor * update + (2.0 * factor_next / half_width) * (residue / diagonal)
            adjoint_field = adjoint_field + update
            factor = factor_next
        return adjoint_field, face_energy(adjoint_field, saved_temp, active)

    costate_temp, thermal_work = lax.map(lone_partial_print, (stored_thermal_state, objective_slope, print_depths))
    slope_rho = (1.0 - FLOOR_COND) * SIMP_POWER * material_share * material_share
    return costate_temp, -slope_rho * jnp.sum(thermal_work, axis=0)
```

```python
import functools

import jax
import jax.numpy as jnp
from jax import lax
from jax.experimental import pallas as pl
from jax.experimental.pallas import tpu as pltpu
from jax.sharding import PartitionSpec as P

SWEEPS = 6
LOSS_RATE = 0.05
FLOOR_COND = 0.001
SIMP_POWER = 3.0
BOUND_LOW = 0.05
BOUND_HIGH = 2.0
CENTER = 0.5 * (BOUND_HIGH + BOUND_LOW)
HALF_WIDTH = 0.5 * (BOUND_HIGH - BOUND_LOW)
MESH = pl.DeviceIdType.MESH
PAD = 8


def factors():
    ratio = CENTER / HALF_WIDTH
    factor = 1.0 / ratio
    table = []
    for _ in range(1, SWEEPS):
        factor_next = 1.0 / (2.0 * ratio - factor)
        table.append((factor_next * factor, 2.0 * factor_next / HALF_WIDTH))
        factor = factor_next
    return table


def pick(index, values):
    out = jnp.float32(values[0])
    for i in range(1, len(values)):
        out = jnp.where(index == i, jnp.float32(values[i]), out)
    return out


def kernel(
    sizes,
    m_ref, t_ref, g_ref, depth_ref, layer_ref,
    adj_ref, sens_ref,
    field, temp, grad, update, inverse, cond, share,
    cxl, cxr, cyu, cyd, cz, part_out, part_in,
    load_sem, store_sem,
    mx_send, mx_recv, mz_send, mz_recv, my_send, my_recv,
    tz_send, tz_recv, ty_send, ty_recv,
    vz_send, vz_recv, vy_send, vy_recv,
    ex_send, ex_recv,
):
    nz, nx, ny, total_planes = sizes
    sections, planes, rows, cols = t_ref.shape
    width = m_ref.shape[2]
    lo, hi = PAD, PAD + rows
    me_z, me_x, me_y = lax.axis_index("slab"), lax.axis_index("section"), lax.axis_index("col")
    body = pl.ds(lo, rows)
    chunk = min(32, rows)
    starts = list(range(0, rows, chunk))

    def xpeer(k):
        return lax.rem(me_x + k, nx)

    zsides = (("slab", me_z > 0, me_z - 1), ("slab", me_z < nz - 1, me_z + 1))
    ysides = (("col", me_y > 0, me_y - 1), ("col", me_y < ny - 1, me_y + 1))

    barrier = pltpu.get_barrier_semaphore()
    count = jnp.int32(nx - 1)
    for k in range(1, nx):
        pl.semaphore_signal(barrier, inc=1, device_id={"section": xpeer(k)}, device_id_type=MESH)
    for name, has, index in zsides + ysides:
        count = count + jnp.where(has, nx, 0)

        @pl.when(has)
        def _():
            for k in range(nx):
                pl.semaphore_signal(
                    barrier, inc=1, device_id={name: index, "section": xpeer(k)}, device_id_type=MESH
                )

    load_m = pltpu.make_async_copy(m_ref, share.at[me_x, pl.ds(1, planes), body], load_sem.at[0])
    load_t = pltpu.make_async_copy(t_ref, temp.at[:, pl.ds(1, planes), body], load_sem.at[1])
    load_g = pltpu.make_async_copy(g_ref, grad, load_sem.at[2])
    load_m.start()
    load_t.start()
    load_g.start()

    for side, (name, has, index) in enumerate(zsides):
        plane = 0 if side == 0 else planes + 1

        @pl.when(jnp.logical_not(has))
        def _():
            for s in range(sections):
                for par in range(2):
                    field[par, s, plane] = jnp.zeros((rows + 2 * PAD, cols), jnp.float32)
                temp[s, plane] = jnp.zeros((rows + 2 * PAD, cols), jnp.float32)
            for k in range(nx):
                share[k, plane] = jnp.zeros((rows + 2 * PAD, width), jnp.float32)

    for side, (name, has, index) in enumerate(ysides):
        first = 0 if side == 0 else hi

        @pl.when(jnp.logical_not(has))
        def _():
            for p in range(1, planes + 1):
                for s in range(sections):
                    for par in range(2):
                        field[par, s, p, first : first + PAD] = jnp.zeros((PAD, cols), jnp.float32)
                    temp[s, p, first : first + PAD] = jnp.zeros((PAD, cols), jnp.float32)
                for k in range(nx):
                    share[k, p, first : first + PAD] = jnp.zeros((PAD, width), jnp.float32)

    pl.semaphore_wait(barrier, count)

    def remote(src, dst, send, recv, device):
        return pltpu.make_async_remote_copy(
            src_ref=src, dst_ref=dst, send_sem=send, recv_sem=recv, device_id=device, device_id_type=MESH
        )

    def mx_copy(k, slot):
        return remote(
            m_ref, share.at[slot, pl.ds(1, planes), body], mx_send.at[k], mx_recv.at[slot],
            {"section": xpeer(k)},
        )

    def mz_copy(side, k, slot):
        src = m_ref.at[0 if side == 0 else planes - 1]
        dst = share.at[slot, planes + 1 if side == 0 else 0, body]
        return remote(
            src, dst, mz_send.at[side, k], mz_recv.at[side, slot],
            {"slab": zsides[side][2], "section": xpeer(k)},
        )

    def my_copy(side, k, slot):
        src = m_ref.at[:, pl.ds(0 if side == 0 else rows - PAD, PAD)]
        dst = share.at[slot, pl.ds(1, planes), pl.ds(hi if side == 0 else 0, PAD)]
        return remote(
            src, dst, my_send.at[side, k], my_recv.at[side, slot],
            {"col": ysides[side][2], "section": xpeer(k)},
        )

    def tz_copy(side):
        src = t_ref.at[:, 0 if side == 0 else planes - 1]
        dst = temp.at[:, planes + 1 if side == 0 else 0, body]
        return remote(src, dst, tz_send.at[side], tz_recv.at[side], {"slab": zsides[side][2]})

    def ty_copy(side):
        src = t_ref.at[:, :, pl.ds(0 if side == 0 else rows - PAD, PAD)]
        dst = temp.at[:, pl.ds(1, planes), pl.ds(hi if side == 0 else 0, PAD)]
        return remote(src, dst, ty_send.at[side], ty_recv.at[side], {"col": ysides[side][2]})

    def vz_copy(side, s, par):
        src = field.at[par, s, 1 if side == 0 else planes, body]
        dst = field.at[par, s, planes + 1 if side == 0 else 0, body]
        return remote(
            src, dst, vz_send.at[side, s, par], vz_recv.at[side, s, par], {"slab": zsides[side][2]}
        )

    spans = [(1, 1), (planes, 1), (2, planes - 2)]

    def vy_copy(side, s, group, par):
        first, number = spans[group]
        src = field.at[par, s, pl.ds(first, number), pl.ds(lo if side == 0 else hi - PAD, PAD)]
        dst = field.at[par, s, pl.ds(first, number), pl.ds(hi if side == 0 else 0, PAD)]
        return remote(
            src, dst, vy_send.at[side, s, group, par], vy_recv.at[side, s, group, par],
            {"col": ysides[side][2]},
        )

    def each(sides, action):
        for side, (name, has, index) in enumerate(sides):
            @pl.when(has)
            def _():
                action(side)

    for k in range(1, nx):
        mx_copy(k, me_x).start()
    each(ysides, lambda side: [my_copy(side, k, me_x).start() for k in range(nx)])
    each(zsides, lambda side: [mz_copy(side, k, me_x).start() for k in range(nx)])
    each(ysides, lambda side: ty_copy(side).start())
    each(zsides, lambda side: tz_copy(side).start())

    def live(s, p):
        plane = me_z * planes - 1 + p
        inside = (plane >= 0) & (plane < total_planes)
        layer = layer_ref[jnp.clip(plane, 0, total_planes - 1)]
        return jnp.where(inside & (layer < depth_ref[s]), jnp.float32(1.0), jnp.float32(0.0))

    active = [[live(s, p) for p in range(planes + 2)] for s in range(sections)]

    load_m.wait()
    for k in range(1, nx):
        mx_copy(k, xpeer(k)).wait_recv()
    each(ysides, lambda side: [my_copy(1 - side, k, k).wait_recv() for k in range(nx)])
    each(zsides, lambda side: [mz_copy(1 - side, k, k).wait_recv() for k in range(nx)])

    def conduct_block(p, r0, number):
        whole = jnp.concatenate([share[k, p, pl.ds(r0, number)] for k in range(nx)], axis=-1)
        cond[p, pl.ds(r0, number)] = 0.5 * (
            FLOOR_COND + (1.0 - FLOOR_COND) * (whole * whole * whole)
        )

    def conduct_plane(p, _):
        for r0 in range(0, rows + 2 * PAD, PAD * 2):
            conduct_block(p, r0, PAD * 2)
        return 0

    lax.fori_loop(1, planes + 1, conduct_plane, 0)
    for p in (0, planes + 1):
        for r0 in starts:
            conduct_block(p, lo + r0, chunk)

    lane = lax.broadcasted_iota(jnp.int32, (chunk, cols), 1)
    row = lax.broadcasted_iota(jnp.int32, (chunk, cols), 0)
    up_mask = jnp.where((row == 0) & (me_y == 0), jnp.float32(0.0), jnp.float32(1.0))
    down_mask = jnp.where((row == chunk - 1) & (me_y == ny - 1), jnp.float32(0.0), jnp.float32(1.0))

    def left(x):
        return pltpu.roll(x, 1, 1)

    def right(x):
        return pltpu.roll(x, cols - 1, 1)

    load_g.wait()

    def setup_chunk(p, r0, act):
        at = pl.ds(r0, chunk)
        h = cond[p, pl.ds(lo + r0, chunk)]
        xl = jnp.where(lane == 0, 0.0, h + left(h))
        xr = jnp.where(lane == cols - 1, 0.0, h + right(h))
        yu = h + cond[p, pl.ds(lo + r0 - 1, chunk)]
        yd = h + cond[p, pl.ds(lo + r0 + 1, chunk)]
        if r0 == 0:
            yu = yu * up_mask
        if r0 == rows - chunk:
            yd = yd * down_mask
        zu = h + cond[p - 1, pl.ds(lo + r0, chunk)]
        zd = h + cond[p + 1, pl.ds(lo + r0, chunk)]
        cxl[p - 1, at] = xl
        cxr[p - 1, at] = xr
        cyu[p - 1, at] = yu
        cyd[p - 1, at] = yd
        cz[p - 1, at] = zu
        cz[p, at] = zd
        flat = (xl + xr) + (yu + yd)
        for s in range(sections):
            above, here, below = act[s]
            diagonal = (LOSS_RATE * here + (1.0 - here)) + here * (flat + above * zu + below * zd)
            inv = here / diagonal
            g = inv * grad[s, p - 1, at]
            inverse[s, p - 1, at] = inv
            grad[s, p - 1, at] = g
            first = g * (1.0 / CENTER)
            update[s, p - 1, at] = first
            field[1, s, p, pl.ds(lo + r0, chunk)] = first

    def start_edges(s, par):
        each(zsides, lambda side: vz_copy(side, s, par).start())
        each(ysides, lambda side: [vy_copy(side, s, group, par).start() for group in (0, 1)])

    def start_inner(s, par):
        if planes > 2:
            each(ysides, lambda side: vy_copy(side, s, 2, par).start())

    def setup_plane(p):
        act = [active[s][p - 1 : p + 2] for s in range(sections)]
        for r0 in starts:
            setup_chunk(p, r0, act)

    setup_plane(1)
    setup_plane(planes)
    for s in range(sections):
        start_edges(s, 1)
    for p in range(2, planes):
        setup_plane(p)
    for s in range(sections):
        start_inner(s, 1)

    table = factors()

    def relax_plane(s, p, now, new, alpha, beta):
        for r0 in starts:
            at = pl.ds(r0, chunk)
            v = field[now, s, p, pl.ds(lo + r0, chunk)]
            total = cxl[p - 1, at] * left(v) + cxr[p - 1, at] * right(v)
            total += cyu[p - 1, at] * field[now, s, p, pl.ds(lo + r0 - 1, chunk)]
            total += cyd[p - 1, at] * field[now, s, p, pl.ds(lo + r0 + 1, chunk)]
            total += cz[p - 1, at] * field[now, s, p - 1, pl.ds(lo + r0, chunk)]
            total += cz[p, at] * field[now, s, p + 1, pl.ds(lo + r0, chunk)]
            u = alpha * update[s, p - 1, at] + beta * (
                (grad[s, p - 1, at] - v) + inverse[s, p - 1, at] * total
            )
            update[s, p - 1, at] = u
            field[new, s, p, pl.ds(lo + r0, chunk)] = v + u

    def sweep(n, _):
        now, new = lax.rem(n - 1, 2), lax.rem(n, 2)
        alpha = pick(n - 2, [a for a, _ in table])
        beta = pick(n - 2, [b for _, b in table])
        for s in range(sections):
            each(zsides, lambda side: vz_copy(1 - side, s, now).wait_recv())
            each(ysides, lambda side: [vy_copy(1 - side, s, group, now).wait_recv() for group in (0, 1)])

            def edge(i, _):
                relax_plane(s, 1 + i * (planes - 1), now, new, alpha, beta)
                return 0

            lax.fori_loop(0, 2, edge, 0)
            start_edges(s, new)
            if planes > 2:
                each(ysides, lambda side: vy_copy(1 - side, s, 2, now).wait_recv())

                def inner(p, _):
                    relax_plane(s, p, now, new, alpha, beta)
                    return 0

                lax.fori_loop(2, planes, inner, 0)
                start_inner(s, new)
                each(ysides, lambda side: vy_copy(side, s, 2, now).wait_send())
            each(zsides, lambda side: vz_copy(side, s, now).wait_send())
            each(ysides, lambda side: [vy_copy(side, s, group, now).wait_send() for group in (0, 1)])
        return 0

    lax.fori_loop(2, SWEEPS + 1, sweep, 0)

    last = SWEEPS % 2
    store = pltpu.make_async_copy(field.at[last, :, pl.ds(1, planes), body], adj_ref, store_sem)
    store.start()

    def ex_copy(k, p, slot):
        return remote(
            part_out.at[slot[0], p - 1], part_in.at[slot[1], p - 1], ex_send.at[k, p - 1],
            ex_recv.at[slot[1], p - 1], {"section": xpeer(k)},
        )

    def energy_plane(p):
        for r0 in starts:
            rest = jnp.zeros((chunk, cols), jnp.float32)
            across = jnp.zeros((chunk, cols), jnp.float32)
            for s in range(sections):
                above, here, below = active[s][p - 1 : p + 2]

                def both(plane, shift):
                    at = pl.ds(lo + r0 + shift, chunk)
                    return field[last, s, plane, at], temp[s, plane, at]

                v, t = both(p, 0)
                across += here * ((v - left(v)) * (t - left(t)))
                v2, t2 = both(p, -1)
                term = (v - v2) * (t - t2)
                if r0 == 0:
                    term = term * up_mask
                v2, t2 = both(p, 1)
                more = (v - v2) * (t - t2)
                if r0 == rows - chunk:
                    more = more * down_mask
                term += more
                v2, t2 = both(p - 1, 0)
                term += above * ((v - v2) * (t - t2))
                v2, t2 = both(p + 1, 0)
                term += below * ((v - v2) * (t - t2))
                rest += here * term
            across = jnp.where(lane == 0, 0.0, across)
            total = 0.5 * (rest + (across + right(across)))
            for k in range(nx):
                part_out[k, p - 1, pl.ds(r0, chunk)] = total[:, k * width : (k + 1) * width]
        for k in range(1, nx):
            ex_copy(k, p, (xpeer(k), me_x)).start()

    each(ysides, lambda side: ty_copy(1 - side).wait_recv())
    load_t.wait()
    for s in range(sections):
        each(ysides, lambda side: [vy_copy(1 - side, s, g, last).wait_recv() for g in (0, 1)])
        if planes > 2:
            each(ysides, lambda side: vy_copy(1 - side, s, 2, last).wait_recv())
    for p in range(2, planes):
        energy_plane(p)
    each(zsides, lambda side: tz_copy(1 - side).wait_recv())
    for s in range(sections):
        each(zsides, lambda side: vz_copy(1 - side, s, last).wait_recv())
    energy_plane(1)
    energy_plane(planes)

    for p in list(range(2, planes)) + [1, planes]:
        for k in range(1, nx):
            ex_copy(k, p, (xpeer(k), xpeer(k))).wait_recv()
        for r0 in starts:
            at = pl.ds(r0, chunk)
            total = part_out[me_x, p - 1, at]
            for k in range(1, nx):
                total += part_in[xpeer(k), p - 1, at]
            m = share[me_x, p, pl.ds(lo + r0, chunk)]
            sens_ref[p - 1, at] = (-(1.0 - FLOOR_COND) * SIMP_POWER) * (m * m) * total

    for k in range(1, nx):
        mx_copy(k, me_x).wait_send()
        for p in range(1, planes + 1):
            ex_copy(k, p, (xpeer(k), me_x)).wait_send()
    each(ysides, lambda side: [my_copy(side, k, me_x).wait_send() for k in range(nx)])
    each(zsides, lambda side: [mz_copy(side, k, me_x).wait_send() for k in range(nx)])
    each(ysides, lambda side: ty_copy(side).wait_send())
    each(zsides, lambda side: tz_copy(side).wait_send())
    for s in range(sections):
        each(zsides, lambda side: vz_copy(side, s, last).wait_send())
        each(ysides, lambda side: [vy_copy(side, s, g, last).wait_send() for g in (0, 1)])
        if planes > 2:
            each(ysides, lambda side: vy_copy(side, s, 2, last).wait_send())
    store.wait()


def solution(mesh):
    nz, nx, ny = mesh.shape["slab"], mesh.shape["section"], mesh.shape["col"]

    def body(material_share, stored_thermal_state, objective_slope, print_depths, slice_to_deposit):
        sections, planes, rows, cols = stored_thermal_state.shape
        width = material_share.shape[2]
        f32 = jnp.float32
        tall = rows + 2 * PAD
        dma = pltpu.SemaphoreType.DMA
        inner = (planes, rows, cols)
        anywhere = pl.BlockSpec(memory_space=pl.ANY)
        return pl.pallas_call(
            functools.partial(kernel, (nz, nx, ny, slice_to_deposit.shape[0])),
            out_shape=(
                jax.ShapeDtypeStruct(stored_thermal_state.shape, f32),
                jax.ShapeDtypeStruct(material_share.shape, f32),
            ),
            in_specs=[anywhere] * 3 + [pl.BlockSpec(memory_space=pltpu.SMEM)] * 2,
            out_specs=(anywhere, pl.BlockSpec(memory_space=pltpu.VMEM)),
            scratch_shapes=[
                pltpu.VMEM((2, sections, planes + 2, tall, cols), f32),
                pltpu.VMEM((sections, planes + 2, tall, cols), f32),
                pltpu.VMEM((sections,) + inner, f32),
                pltpu.VMEM((sections,) + inner, f32),
                pltpu.VMEM((sections,) + inner, f32),
                pltpu.VMEM((planes + 2, tall, cols), f32),
                pltpu.VMEM((nx, planes + 2, tall, width), f32),
                pltpu.VMEM(inner, f32),
                pltpu.VMEM(inner, f32),
                pltpu.VMEM(inner, f32),
                pltpu.VMEM(inner, f32),
                pltpu.VMEM((planes + 1, rows, cols), f32),
                pltpu.VMEM((nx, planes, rows, width), f32),
                pltpu.VMEM((nx, planes, rows, width), f32),
                dma((3,)),
                dma(()),
                dma((nx,)), dma((nx,)),
                dma((2, nx)), dma((2, nx)),
                dma((2, nx)), dma((2, nx)),
                dma((2,)), dma((2,)),
                dma((2,)), dma((2,)),
                dma((2, sections, 2)), dma((2, sections, 2)),
                dma((2, sections, 3, 2)), dma((2, sections, 3, 2)),
                dma((nx, planes)), dma((nx, planes)),
            ],
            compiler_params=pltpu.CompilerParams(
                collective_id=0, has_side_effects=True, vmem_limit_bytes=40 * 1024 * 1024
            ),
        )(material_share, stored_thermal_state, objective_slope, print_depths, slice_to_deposit)

    return jax.shard_map(
        body,
        mesh=mesh,
        in_specs=(
            P(("parts", "slab"), "col", "section"),
            P(("parts", "section"), "slab", "col", None),
            P(("parts", "section"), "slab", "col", None),
            P(("parts", "section")),
            P("parts"),
        ),
        out_specs=(
            P(("parts", "section"), "slab", "col", None),
            P(("parts", "slab"), "col", "section"),
        ),
        check_vma=False,
    )
```

```python
import functools

import jax
import jax.numpy as jnp
from jax import lax
from jax.experimental import pallas as pl
from jax.experimental.pallas import tpu as pltpu
from jax.sharding import PartitionSpec as P

SWEEPS = 6
LOSS_RATE = 0.05
FLOOR_COND = 0.001
SIMP_POWER = 3.0
BOUND_LOW = 0.05
BOUND_HIGH = 2.0
CENTER = 0.5 * (BOUND_HIGH + BOUND_LOW)
HALF_WIDTH = 0.5 * (BOUND_HIGH - BOUND_LOW)
MESH = pl.DeviceIdType.MESH
PAD = 8


def factors():
    ratio = CENTER / HALF_WIDTH
    factor = 1.0 / ratio
    table = []
    for _ in range(1, SWEEPS):
        factor_next = 1.0 / (2.0 * ratio - factor)
        table.append((factor_next * factor, 2.0 * factor_next / HALF_WIDTH))
        factor = factor_next
    return table


def kernel(
    sizes,
    m_ref, t_ref, g_ref, depth_ref, layer_ref,
    adj_ref, sens_ref,
    even, odd, temp, grad, update, inverse, cond, share,
    cxl, cxr, cyu, cyd, cz, part_out, part_in,
    load_sem, store_sem,
    mx_send, mx_recv, mz_send, mz_recv, my_send, my_recv,
    tz_send, tz_recv, ty_send, ty_recv,
    vz_send, vz_recv, vy_send, vy_recv,
    ex_send, ex_recv,
):
    nz, nx, ny, total_planes = sizes
    sections, planes, rows, cols = t_ref.shape
    width = m_ref.shape[2]
    fields = (even, odd)
    lanes = even.shape[-1]
    parts = cols // lanes
    halves = range(parts)
    lo, hi = PAD, PAD + rows
    me_z, me_x, me_y = lax.axis_index("slab"), lax.axis_index("section"), lax.axis_index("col")
    body = pl.ds(lo, rows)
    chunk = min(32, rows)
    starts = list(range(0, rows, chunk))

    def xpeer(k):
        return lax.rem(me_x + k, nx)

    zsides = (("slab", me_z > 0, me_z - 1), ("slab", me_z < nz - 1, me_z + 1))
    ysides = (("col", me_y > 0, me_y - 1), ("col", me_y < ny - 1, me_y + 1))

    barrier = pltpu.get_barrier_semaphore()
    count = jnp.int32(nx - 1)
    for k in range(1, nx):
        pl.semaphore_signal(barrier, inc=1, device_id={"section": xpeer(k)}, device_id_type=MESH)
    for name, has, index in zsides + ysides:
        count = count + jnp.where(has, nx, 0)

        @pl.when(has)
        def _():
            for k in range(nx):
                pl.semaphore_signal(
                    barrier, inc=1, device_id={name: index, "section": xpeer(k)}, device_id_type=MESH
                )

    load_m = pltpu.make_async_copy(m_ref, share.at[me_x, pl.ds(1, planes), body], load_sem.at[0])
    load_t = [
        pltpu.make_async_copy(
            t_ref.at[:, :, :, pl.ds(h * lanes, lanes)], temp.at[:, pl.ds(1, planes), h, body],
            load_sem.at[1 + h],
        )
        for h in halves
    ]
    load_g = [
        pltpu.make_async_copy(
            g_ref.at[:, :, :, pl.ds(h * lanes, lanes)], grad.at[:, :, h], load_sem.at[1 + parts + h]
        )
        for h in halves
    ]
    for load in [load_m] + load_t + load_g:
        load.start()

    for side, (name, has, index) in enumerate(zsides):
        plane = 0 if side == 0 else planes + 1

        @pl.when(jnp.logical_not(has))
        def _():
            for s in range(sections):
                for par in range(2):
                    fields[par][s, plane] = jnp.zeros(even.shape[2:], jnp.float32)
                temp[s, plane] = jnp.zeros(temp.shape[2:], jnp.float32)
            for k in range(nx):
                share[k, plane] = jnp.zeros((rows + 2 * PAD, width), jnp.float32)

    for side, (name, has, index) in enumerate(ysides):
        first = 0 if side == 0 else hi

        @pl.when(jnp.logical_not(has))
        def _():
            for p in range(1, planes + 1):
                for s in range(sections):
                    for par in range(2):
                        fields[par][s, p, :, first : first + PAD] = jnp.zeros((parts, PAD, lanes), jnp.float32)
                    temp[s, p, :, first : first + PAD] = jnp.zeros((parts, PAD, lanes), jnp.float32)
                for k in range(nx):
                    share[k, p, first : first + PAD] = jnp.zeros((PAD, width), jnp.float32)

    pl.semaphore_wait(barrier, count)

    def remote(src, dst, send, recv, device):
        return pltpu.make_async_remote_copy(
            src_ref=src, dst_ref=dst, send_sem=send, recv_sem=recv, device_id=device, device_id_type=MESH
        )

    def mx_copy(k, slot):
        return remote(
            m_ref, share.at[slot, pl.ds(1, planes), body], mx_send.at[k], mx_recv.at[slot],
            {"section": xpeer(k)},
        )

    def mz_copy(side, k, slot):
        src = m_ref.at[0 if side == 0 else planes - 1]
        dst = share.at[slot, planes + 1 if side == 0 else 0, body]
        return remote(
            src, dst, mz_send.at[side, k], mz_recv.at[side, slot],
            {"slab": zsides[side][2], "section": xpeer(k)},
        )

    def my_copy(side, k, slot):
        src = m_ref.at[:, pl.ds(0 if side == 0 else rows - PAD, PAD)]
        dst = share.at[slot, pl.ds(1, planes), pl.ds(hi if side == 0 else 0, PAD)]
        return remote(
            src, dst, my_send.at[side, k], my_recv.at[side, slot],
            {"col": ysides[side][2], "section": xpeer(k)},
        )

    def tz_copy(side):
        src = temp.at[:, 1 if side == 0 else planes, :, body]
        dst = temp.at[:, planes + 1 if side == 0 else 0, :, body]
        return remote(src, dst, tz_send.at[side], tz_recv.at[side], {"slab": zsides[side][2]})

    def ty_copy(side):
        src = temp.at[:, pl.ds(1, planes), :, pl.ds(lo if side == 0 else hi - PAD, PAD)]
        dst = temp.at[:, pl.ds(1, planes), :, pl.ds(hi if side == 0 else 0, PAD)]
        return remote(src, dst, ty_send.at[side], ty_recv.at[side], {"col": ysides[side][2]})

    def vz_copy(side, s, par):
        src = fields[par].at[s, 1 if side == 0 else planes, :, body]
        dst = fields[par].at[s, planes + 1 if side == 0 else 0, :, body]
        return remote(
            src, dst, vz_send.at[side, s, par], vz_recv.at[side, s, par], {"slab": zsides[side][2]}
        )

    spans = [(1, 1), (planes, 1), (2, planes - 2)]

    def vy_copy(side, s, group, par):
        first, number = spans[group]
        src = fields[par].at[s, pl.ds(first, number), :, pl.ds(lo if side == 0 else hi - PAD, PAD)]
        dst = fields[par].at[s, pl.ds(first, number), :, pl.ds(hi if side == 0 else 0, PAD)]
        return remote(
            src, dst, vy_send.at[side, s, group, par], vy_recv.at[side, s, group, par],
            {"col": ysides[side][2]},
        )

    def each(sides, action):
        for side, (name, has, index) in enumerate(sides):
            @pl.when(has)
            def _():
                action(side)

    for k in range(1, nx):
        mx_copy(k, me_x).start()
    each(ysides, lambda side: [my_copy(side, k, me_x).start() for k in range(nx)])
    each(zsides, lambda side: [mz_copy(side, k, me_x).start() for k in range(nx)])
    for load in load_t:
        load.wait()
    each(ysides, lambda side: ty_copy(side).start())
    each(zsides, lambda side: tz_copy(side).start())

    def live(s, p):
        plane = me_z * planes - 1 + p
        inside = (plane >= 0) & (plane < total_planes)
        layer = layer_ref[jnp.clip(plane, 0, total_planes - 1)]
        return jnp.where(inside & (layer < depth_ref[s]), jnp.float32(1.0), jnp.float32(0.0))

    active = [[live(s, p) for p in range(planes + 2)] for s in range(sections)]

    load_m.wait()
    for k in range(1, nx):
        mx_copy(k, xpeer(k)).wait_recv()
    each(ysides, lambda side: [my_copy(1 - side, k, k).wait_recv() for k in range(nx)])
    each(zsides, lambda side: [mz_copy(1 - side, k, k).wait_recv() for k in range(nx)])

    def conduct_block(p, r0, number):
        whole = jnp.concatenate([share[k, p, pl.ds(r0, number)] for k in range(nx)], axis=-1)
        whole = 0.5 * (FLOOR_COND + (1.0 - FLOOR_COND) * (whole * whole * whole))
        for h in halves:
            cond[p, h, pl.ds(r0, number)] = whole[:, h * lanes : (h + 1) * lanes]

    def conduct_plane(p, _):
        for r0 in range(0, rows + 2 * PAD, PAD * 2):
            conduct_block(p, r0, PAD * 2)
        return 0

    lax.fori_loop(1, planes + 1, conduct_plane, 0)
    for p in (0, planes + 1):
        for r0 in starts:
            conduct_block(p, lo + r0, chunk)

    lane = lax.broadcasted_iota(jnp.int32, (chunk, lanes), 1)
    row = lax.broadcasted_iota(jnp.int32, (chunk, lanes), 0)
    up_mask = jnp.where((row == 0) & (me_y == 0), jnp.float32(0.0), jnp.float32(1.0))
    down_mask = jnp.where((row == chunk - 1) & (me_y == ny - 1), jnp.float32(0.0), jnp.float32(1.0))

    def left(xs):
        turned = [pltpu.roll(x, 1, 1) for x in xs]
        return [turned[0]] + [jnp.where(lane == 0, turned[h - 1], turned[h]) for h in halves[1:]]

    def right(xs):
        turned = [pltpu.roll(x, lanes - 1, 1) for x in xs]
        return [
            jnp.where(lane == lanes - 1, turned[h + 1], turned[h]) for h in halves[:-1]
        ] + [turned[-1]]

    for load in load_g:
        load.wait()

    def setup_chunk(p, r0, act):
        at = pl.ds(r0, chunk)
        hs = [cond[p, h, pl.ds(lo + r0, chunk)] for h in halves]
        hl, hr = left(hs), right(hs)
        for h in halves:
            here_h = hs[h]
            xl = here_h + hl[h]
            xr = here_h + hr[h]
            if h == 0:
                xl = jnp.where(lane == 0, 0.0, xl)
            if h == parts - 1:
                xr = jnp.where(lane == lanes - 1, 0.0, xr)
            yu = here_h + cond[p, h, pl.ds(lo + r0 - 1, chunk)]
            yd = here_h + cond[p, h, pl.ds(lo + r0 + 1, chunk)]
            if r0 == 0:
                yu = yu * up_mask
            if r0 == rows - chunk:
                yd = yd * down_mask
            zu = here_h + cond[p - 1, h, pl.ds(lo + r0, chunk)]
            zd = here_h + cond[p + 1, h, pl.ds(lo + r0, chunk)]
            cxl[p - 1, h, at] = xl
            cxr[p - 1, h, at] = xr
            cyu[p - 1, h, at] = yu
            cyd[p - 1, h, at] = yd
            cz[p - 1, h, at] = zu
            cz[p, h, at] = zd
            flat = (xl + xr) + (yu + yd)
            for s in range(sections):
                above, here, below = act[s]
                diagonal = (LOSS_RATE * here + (1.0 - here)) + here * (
                    flat + above * zu + below * zd
                )
                inv = here / diagonal
                g = inv * grad[s, p - 1, h, at]
                inverse[s, p - 1, h, at] = inv
                grad[s, p - 1, h, at] = g
                first = g * (1.0 / CENTER)
                update[s, p - 1, h, at] = first
                odd[s, p, h, pl.ds(lo + r0, chunk)] = first

    def start_edges(s, par):
        each(zsides, lambda side: vz_copy(side, s, par).start())
        each(ysides, lambda side: [vy_copy(side, s, group, par).start() for group in (0, 1)])

    def start_inner(s, par):
        if planes > 2:
            each(ysides, lambda side: vy_copy(side, s, 2, par).start())

    def setup_plane(p):
        act = [active[s][p - 1 : p + 2] for s in range(sections)]
        for r0 in starts:
            setup_chunk(p, r0, act)

    setup_plane(1)
    setup_plane(planes)
    for s in range(sections):
        start_edges(s, 1)
    for p in range(2, planes):
        setup_plane(p)
    for s in range(sections):
        start_inner(s, 1)

    table = factors()

    def relax_plane(s, p, now, new, alpha, beta):
        for r0 in starts:
            at = pl.ds(r0, chunk)
            mid = pl.ds(lo + r0, chunk)
            vs = [now[s, p, h, mid] for h in halves]
            vl, vr = left(vs), right(vs)
            for h in halves:
                v = vs[h]
                total = cxl[p - 1, h, at] * vl[h] + cxr[p - 1, h, at] * vr[h]
                total += cyu[p - 1, h, at] * now[s, p, h, pl.ds(lo + r0 - 1, chunk)]
                total += cyd[p - 1, h, at] * now[s, p, h, pl.ds(lo + r0 + 1, chunk)]
                total += cz[p - 1, h, at] * now[s, p - 1, h, mid]
                total += cz[p, h, at] * now[s, p + 1, h, mid]
                u = alpha * update[s, p - 1, h, at] + beta * (
                    (grad[s, p - 1, h, at] - v) + inverse[s, p - 1, h, at] * total
                )
                update[s, p - 1, h, at] = u
                new[s, p, h, mid] = v + u

    for n in range(2, SWEEPS + 1):
        now, new = (n - 1) % 2, n % 2
        for s in range(sections):
            relax = functools.partial(
                relax_plane, now=fields[now], new=fields[new], alpha=table[n - 2][0], beta=table[n - 2][1]
            )
            each(zsides, lambda side: vz_copy(1 - side, s, now).wait_recv())
            each(ysides, lambda side: [vy_copy(1 - side, s, group, now).wait_recv() for group in (0, 1)])

            def edge(i, _):
                relax(s, 1 + i * (planes - 1))
                return 0

            lax.fori_loop(0, 2, edge, 0)
            start_edges(s, new)
            if planes > 2:
                each(ysides, lambda side: vy_copy(1 - side, s, 2, now).wait_recv())

                def inner(p, _):
                    relax(s, p)
                    return 0

                lax.fori_loop(2, planes, inner, 0)
                start_inner(s, new)
                each(ysides, lambda side: vy_copy(side, s, 2, now).wait_send())
            each(zsides, lambda side: vz_copy(side, s, now).wait_send())
            each(ysides, lambda side: [vy_copy(side, s, group, now).wait_send() for group in (0, 1)])

    last = SWEEPS % 2
    stores = [
        pltpu.make_async_copy(
            fields[last].at[:, pl.ds(1, planes), h, body],
            adj_ref.at[:, :, :, pl.ds(h * lanes, lanes)], store_sem.at[h],
        )
        for h in halves
    ]
    for store in stores:
        store.start()

    def ex_copy(k, p, slot):
        return remote(
            part_out.at[slot[0], p - 1], part_in.at[slot[1], p - 1], ex_send.at[k, p - 1],
            ex_recv.at[slot[1], p - 1], {"section": xpeer(k)},
        )

    def energy_plane(p):
        for r0 in starts:
            rest = [0.0] * parts
            across = [0.0] * parts
            for s in range(sections):
                above, here, below = active[s][p - 1 : p + 2]

                def both(plane, h, shift):
                    at = pl.ds(lo + r0 + shift, chunk)
                    return fields[last][s, plane, h, at], temp[s, plane, h, at]

                pairs = [both(p, h, 0) for h in halves]
                vl, tl = left([v for v, _ in pairs]), left([t for _, t in pairs])
                for h in halves:
                    v, t = pairs[h]
                    across[h] += here * ((v - vl[h]) * (t - tl[h]))
                    v2, t2 = both(p, h, -1)
                    term = (v - v2) * (t - t2)
                    if r0 == 0:
                        term = term * up_mask
                    v2, t2 = both(p, h, 1)
                    more = (v - v2) * (t - t2)
                    if r0 == rows - chunk:
                        more = more * down_mask
                    term += more
                    v2, t2 = both(p - 1, h, 0)
                    term += above * ((v - v2) * (t - t2))
                    v2, t2 = both(p + 1, h, 0)
                    term += below * ((v - v2) * (t - t2))
                    rest[h] += here * term
            across[0] = jnp.where(lane == 0, 0.0, across[0])
            beyond = right(across)
            beyond[-1] = jnp.where(lane == lanes - 1, 0.0, beyond[-1])
            totals = [0.5 * (rest[h] + (across[h] + beyond[h])) for h in halves]
            if width != lanes:
                total = jnp.concatenate(totals, axis=-1)
                totals = [total[:, k * width : (k + 1) * width] for k in range(nx)]
            for k in range(nx):
                part_out[k, p - 1, pl.ds(r0, chunk)] = totals[k]
        for k in range(1, nx):
            ex_copy(k, p, (xpeer(k), me_x)).start()

    each(ysides, lambda side: ty_copy(1 - side).wait_recv())
    for s in range(sections):
        each(ysides, lambda side: [vy_copy(1 - side, s, g, last).wait_recv() for g in (0, 1)])
        if planes > 2:
            each(ysides, lambda side: vy_copy(1 - side, s, 2, last).wait_recv())
    for p in range(2, planes):
        energy_plane(p)
    each(zsides, lambda side: tz_copy(1 - side).wait_recv())
    for s in range(sections):
        each(zsides, lambda side: vz_copy(1 - side, s, last).wait_recv())
    energy_plane(1)
    energy_plane(planes)

    for p in list(range(2, planes)) + [1, planes]:
        for k in range(1, nx):
            ex_copy(k, p, (xpeer(k), xpeer(k))).wait_recv()
        for r0 in starts:
            at = pl.ds(r0, chunk)
            total = part_out[me_x, p - 1, at]
            for k in range(1, nx):
                total += part_in[xpeer(k), p - 1, at]
            m = share[me_x, p, pl.ds(lo + r0, chunk)]
            sens_ref[p - 1, at] = (-(1.0 - FLOOR_COND) * SIMP_POWER) * (m * m) * total

    for k in range(1, nx):
        mx_copy(k, me_x).wait_send()
        for p in range(1, planes + 1):
            ex_copy(k, p, (xpeer(k), me_x)).wait_send()
    each(ysides, lambda side: [my_copy(side, k, me_x).wait_send() for k in range(nx)])
    each(zsides, lambda side: [mz_copy(side, k, me_x).wait_send() for k in range(nx)])
    each(ysides, lambda side: ty_copy(side).wait_send())
    each(zsides, lambda side: tz_copy(side).wait_send())
    for s in range(sections):
        each(zsides, lambda side: vz_copy(side, s, last).wait_send())
        each(ysides, lambda side: [vy_copy(side, s, g, last).wait_send() for g in (0, 1)])
        if planes > 2:
            each(ysides, lambda side: vy_copy(side, s, 2, last).wait_send())
    for store in stores:
        store.wait()


def solution(mesh):
    nz, nx, ny = mesh.shape["slab"], mesh.shape["section"], mesh.shape["col"]

    def body(material_share, stored_thermal_state, objective_slope, print_depths, slice_to_deposit):
        sections, planes, rows, cols = stored_thermal_state.shape
        width = material_share.shape[2]
        f32 = jnp.float32
        tall = rows + 2 * PAD
        dma = pltpu.SemaphoreType.DMA
        lanes = 128 if cols % 128 == 0 else cols
        split = cols // lanes
        inner = (planes, split, rows, lanes)
        anywhere = pl.BlockSpec(memory_space=pltpu.HBM)
        return pl.pallas_call(
            functools.partial(kernel, (nz, nx, ny, slice_to_deposit.shape[0])),
            out_shape=(
                jax.ShapeDtypeStruct(stored_thermal_state.shape, f32),
                jax.ShapeDtypeStruct(material_share.shape, f32),
            ),
            in_specs=[anywhere] * 3 + [pl.BlockSpec(memory_space=pltpu.SMEM)] * 2,
            out_specs=(anywhere, pl.BlockSpec(memory_space=pltpu.VMEM)),
            scratch_shapes=[
                pltpu.VMEM((sections, planes + 2, split, tall, lanes), f32),
                pltpu.VMEM((sections, planes + 2, split, tall, lanes), f32),
                pltpu.VMEM((sections, planes + 2, split, tall, lanes), f32),
                pltpu.VMEM((sections,) + inner, f32),
                pltpu.VMEM((sections,) + inner, f32),
                pltpu.VMEM((sections,) + inner, f32),
                pltpu.VMEM((planes + 2, split, tall, lanes), f32),
                pltpu.VMEM((nx, planes + 2, tall, width), f32),
                pltpu.VMEM(inner, f32),
                pltpu.VMEM(inner, f32),
                pltpu.VMEM(inner, f32),
                pltpu.VMEM(inner, f32),
                pltpu.VMEM((planes + 1, split, rows, lanes), f32),
                pltpu.VMEM((nx, planes, rows, width), f32),
                pltpu.VMEM((nx, planes, rows, width), f32),
                dma((1 + 2 * split,)),
                dma((split,)),
                dma((nx,)), dma((nx,)),
                dma((2, nx)), dma((2, nx)),
                dma((2, nx)), dma((2, nx)),
                dma((2,)), dma((2,)),
                dma((2,)), dma((2,)),
                dma((2, sections, 2)), dma((2, sections, 2)),
                dma((2, sections, 3, 2)), dma((2, sections, 3, 2)),
                dma((nx, planes)), dma((nx, planes)),
            ],
            compiler_params=pltpu.CompilerParams(
                collective_id=0, has_side_effects=True, vmem_limit_bytes=63 * 1024 * 1024
            ),
        )(material_share, stored_thermal_state, objective_slope, print_depths, slice_to_deposit)

    return jax.shard_map(
        body,
        mesh=mesh,
        in_specs=(
            P(("parts", "slab"), "col", "section"),
            P(("parts", "section"), "slab", "col", None),
            P(("parts", "section"), "slab", "col", None),
            P(("parts", "section")),
            P("parts"),
        ),
        out_specs=(
            P(("parts", "section"), "slab", "col", None),
            P(("parts", "slab"), "col", "section"),
        ),
        check_vma=False,
    )
```

```python
import functools

import jax
import jax.numpy as jnp
from jax import lax
from jax.experimental import pallas as pl
from jax.experimental.pallas import tpu as pltpu
from jax.sharding import PartitionSpec as P

SWEEPS = 6
LOSS_RATE = 0.05
FLOOR_COND = 0.001
SIMP_POWER = 3.0
BOUND_LOW = 0.05
BOUND_HIGH = 2.0
CENTER = 0.5 * (BOUND_HIGH + BOUND_LOW)
HALF_WIDTH = 0.5 * (BOUND_HIGH - BOUND_LOW)
MESH = pl.DeviceIdType.MESH
PAD = 8


def factors():
    ratio = CENTER / HALF_WIDTH
    factor = 1.0 / ratio
    table = []
    for _ in range(1, SWEEPS):
        factor_next = 1.0 / (2.0 * ratio - factor)
        table.append((factor_next * factor, 2.0 * factor_next / HALF_WIDTH))
        factor = factor_next
    return table


def kernel(
    sizes,
    m_ref, t_ref, g_ref, depth_ref, layer_ref,
    adj_ref, sens_ref,
    even, odd, temp, grad, update, inverse, cond, share,
    cxl, cxr, cyu, cyd, cz, part_out, part_in,
    load_sem, store_sem,
    mx_send, mx_recv, mz_send, mz_recv, my_send, my_recv,
    tz_send, tz_recv, ty_send, ty_recv,
    vz_send, vz_recv, vy_send, vy_recv,
    ex_send, ex_recv, eq_send, eq_recv, vq_send, vq_recv,
):
    nz, nx, ny, total_planes = sizes
    sections, planes, rows, cols = t_ref.shape
    width = m_ref.shape[2]
    fields = (even, odd)
    lanes = even.shape[-1]
    parts = cols // lanes
    halves = range(parts)
    lo, hi = PAD, PAD + rows
    me_z, me_x, me_y = lax.axis_index("slab"), lax.axis_index("section"), lax.axis_index("col")
    body = pl.ds(lo, rows)
    chunk = min(32, rows)
    starts = list(range(0, rows, chunk))

    def xpeer(k):
        return lax.rem(me_x + k, nx)

    zsides = (("slab", me_z > 0, me_z - 1), ("slab", me_z < nz - 1, me_z + 1))
    ysides = (("col", me_y > 0, me_y - 1), ("col", me_y < ny - 1, me_y + 1))

    barrier = pltpu.get_barrier_semaphore()
    count = jnp.int32(nx - 1)
    for k in range(1, nx):
        pl.semaphore_signal(barrier, inc=1, device_id={"section": xpeer(k)}, device_id_type=MESH)
    for name, has, index in zsides + ysides:
        count = count + jnp.where(has, nx, 0)

        @pl.when(has)
        def _():
            for k in range(nx):
                pl.semaphore_signal(
                    barrier, inc=1, device_id={name: index, "section": xpeer(k)}, device_id_type=MESH
                )

    load_m = pltpu.make_async_copy(m_ref, share.at[me_x, pl.ds(1, planes), body], load_sem.at[0])
    load_t = [
        pltpu.make_async_copy(
            t_ref.at[:, :, :, pl.ds(h * lanes, lanes)], temp.at[:, pl.ds(1, planes), h, body],
            load_sem.at[1 + h],
        )
        for h in halves
    ]
    load_g = [
        pltpu.make_async_copy(
            g_ref.at[:, :, :, pl.ds(h * lanes, lanes)], grad.at[:, :, h], load_sem.at[1 + parts + h]
        )
        for h in halves
    ]
    for load in [load_m] + load_t + load_g:
        load.start()

    for side, (name, has, index) in enumerate(zsides):
        plane = 0 if side == 0 else planes + 1

        @pl.when(jnp.logical_not(has))
        def _():
            for s in range(sections):
                for par in range(2):
                    fields[par][s, plane] = jnp.zeros(even.shape[2:], jnp.float32)
                temp[s, plane] = jnp.zeros(temp.shape[2:], jnp.float32)
            for k in range(nx):
                share[k, plane] = jnp.zeros((rows + 2 * PAD, width), jnp.float32)

    for side, (name, has, index) in enumerate(ysides):
        first = 0 if side == 0 else hi

        @pl.when(jnp.logical_not(has))
        def _():
            for p in range(1, planes + 1):
                for s in range(sections):
                    for par in range(2):
                        fields[par][s, p, :, first : first + PAD] = jnp.zeros((parts, PAD, lanes), jnp.float32)
                    temp[s, p, :, first : first + PAD] = jnp.zeros((parts, PAD, lanes), jnp.float32)
                for k in range(nx):
                    share[k, p, first : first + PAD] = jnp.zeros((PAD, width), jnp.float32)

    pl.semaphore_wait(barrier, count)

    def remote(src, dst, send, recv, device):
        return pltpu.make_async_remote_copy(
            src_ref=src, dst_ref=dst, send_sem=send, recv_sem=recv, device_id=device, device_id_type=MESH
        )

    def mx_copy(k, slot):
        return remote(
            m_ref, share.at[slot, pl.ds(1, planes), body], mx_send.at[k], mx_recv.at[slot],
            {"section": xpeer(k)},
        )

    def mz_copy(side, k, slot):
        src = m_ref.at[0 if side == 0 else planes - 1]
        dst = share.at[slot, planes + 1 if side == 0 else 0, body]
        return remote(
            src, dst, mz_send.at[side, k], mz_recv.at[side, slot],
            {"slab": zsides[side][2], "section": xpeer(k)},
        )

    def my_copy(side, k, slot):
        src = m_ref.at[:, pl.ds(0 if side == 0 else rows - PAD, PAD)]
        dst = share.at[slot, pl.ds(1, planes), pl.ds(hi if side == 0 else 0, PAD)]
        return remote(
            src, dst, my_send.at[side, k], my_recv.at[side, slot],
            {"col": ysides[side][2], "section": xpeer(k)},
        )

    def tz_copy(side):
        src = temp.at[:, 1 if side == 0 else planes, :, body]
        dst = temp.at[:, planes + 1 if side == 0 else 0, :, body]
        return remote(src, dst, tz_send.at[side], tz_recv.at[side], {"slab": zsides[side][2]})

    def ty_copy(side):
        src = temp.at[:, pl.ds(1, planes), :, pl.ds(lo if side == 0 else hi - PAD, PAD)]
        dst = temp.at[:, pl.ds(1, planes), :, pl.ds(hi if side == 0 else 0, PAD)]
        return remote(src, dst, ty_send.at[side], ty_recv.at[side], {"col": ysides[side][2]})

    def vz_copy(side, s, par):
        src = fields[par].at[s, 1 if side == 0 else planes, :, body]
        dst = fields[par].at[s, planes + 1 if side == 0 else 0, :, body]
        return remote(
            src, dst, vz_send.at[side, s, par], vz_recv.at[side, s, par], {"slab": zsides[side][2]}
        )

    def vq_copy(side, q):
        here = fields[SWEEPS % 2].at[sections - 1, :, :, pl.ds(lo + starts[q], chunk)]
        return remote(
            here.at[1 if side == 0 else planes], here.at[planes + 1 if side == 0 else 0],
            vq_send.at[side, q], vq_recv.at[side, q], {"slab": zsides[side][2]},
        )

    spans = [(1, 1), (planes, 1), (2, planes - 2)]

    def vy_copy(side, s, group, par):
        first, number = spans[group]
        src = fields[par].at[s, pl.ds(first, number), :, pl.ds(lo if side == 0 else hi - PAD, PAD)]
        dst = fields[par].at[s, pl.ds(first, number), :, pl.ds(hi if side == 0 else 0, PAD)]
        return remote(
            src, dst, vy_send.at[side, s, group, par], vy_recv.at[side, s, group, par],
            {"col": ysides[side][2]},
        )

    def each(sides, action):
        for side, (name, has, index) in enumerate(sides):
            @pl.when(has)
            def _():
                action(side)

    for k in range(1, nx):
        mx_copy(k, me_x).start()
    each(ysides, lambda side: [my_copy(side, k, me_x).start() for k in range(nx)])
    each(zsides, lambda side: [mz_copy(side, k, me_x).start() for k in range(nx)])
    for load in load_t:
        load.wait()
    each(ysides, lambda side: ty_copy(side).start())
    each(zsides, lambda side: tz_copy(side).start())

    def live(s, p):
        plane = me_z * planes - 1 + p
        inside = (plane >= 0) & (plane < total_planes)
        layer = layer_ref[jnp.clip(plane, 0, total_planes - 1)]
        return jnp.where(inside & (layer < depth_ref[s]), jnp.float32(1.0), jnp.float32(0.0))

    active = [[live(s, p) for p in range(planes + 2)] for s in range(sections)]

    load_m.wait()
    for k in range(1, nx):
        mx_copy(k, xpeer(k)).wait_recv()
    each(ysides, lambda side: [my_copy(1 - side, k, k).wait_recv() for k in range(nx)])
    each(zsides, lambda side: [mz_copy(1 - side, k, k).wait_recv() for k in range(nx)])

    def conduct_block(p, r0, number):
        whole = jnp.concatenate([share[k, p, pl.ds(r0, number)] for k in range(nx)], axis=-1)
        whole = 0.5 * (FLOOR_COND + (1.0 - FLOOR_COND) * (whole * whole * whole))
        for h in halves:
            cond[p, h, pl.ds(r0, number)] = whole[:, h * lanes : (h + 1) * lanes]

    def conduct_plane(p, _):
        for r0 in range(0, rows + 2 * PAD, PAD * 2):
            conduct_block(p, r0, PAD * 2)
        return 0

    lax.fori_loop(1, planes + 1, conduct_plane, 0)
    for p in (0, planes + 1):
        for r0 in starts:
            conduct_block(p, lo + r0, chunk)

    lane = lax.broadcasted_iota(jnp.int32, (chunk, lanes), 1)
    row = lax.broadcasted_iota(jnp.int32, (chunk, lanes), 0)
    up_mask = jnp.where((row == 0) & (me_y == 0), jnp.float32(0.0), jnp.float32(1.0))
    down_mask = jnp.where((row == chunk - 1) & (me_y == ny - 1), jnp.float32(0.0), jnp.float32(1.0))

    def left(xs):
        turned = [pltpu.roll(x, 1, 1) for x in xs]
        return [turned[0]] + [jnp.where(lane == 0, turned[h - 1], turned[h]) for h in halves[1:]]

    def right(xs):
        turned = [pltpu.roll(x, lanes - 1, 1) for x in xs]
        return [
            jnp.where(lane == lanes - 1, turned[h + 1], turned[h]) for h in halves[:-1]
        ] + [turned[-1]]

    for load in load_g:
        load.wait()

    def setup_chunk(p, r0, act):
        at = pl.ds(r0, chunk)
        hs = [cond[p, h, pl.ds(lo + r0, chunk)] for h in halves]
        hl, hr = left(hs), right(hs)
        for h in halves:
            here_h = hs[h]
            xl = here_h + hl[h]
            xr = here_h + hr[h]
            if h == 0:
                xl = jnp.where(lane == 0, 0.0, xl)
            if h == parts - 1:
                xr = jnp.where(lane == lanes - 1, 0.0, xr)
            yu = here_h + cond[p, h, pl.ds(lo + r0 - 1, chunk)]
            yd = here_h + cond[p, h, pl.ds(lo + r0 + 1, chunk)]
            if r0 == 0:
                yu = yu * up_mask
            if r0 == rows - chunk:
                yd = yd * down_mask
            zu = here_h + cond[p - 1, h, pl.ds(lo + r0, chunk)]
            zd = here_h + cond[p + 1, h, pl.ds(lo + r0, chunk)]
            cxl[p - 1, h, at] = xl
            cxr[p - 1, h, at] = xr
            cyu[p - 1, h, at] = yu
            cyd[p - 1, h, at] = yd
            cz[p - 1, h, at] = zu
            cz[p, h, at] = zd
            flat = (xl + xr) + (yu + yd)
            for s in range(sections):
                above, here, below = act[s]
                diagonal = (LOSS_RATE * here + (1.0 - here)) + here * (
                    flat + above * zu + below * zd
                )
                inv = here / diagonal
                g = inv * grad[s, p - 1, h, at]
                inverse[s, p - 1, h, at] = inv
                grad[s, p - 1, h, at] = g
                first = g * (1.0 / CENTER)
                update[s, p - 1, h, at] = first
                odd[s, p, h, pl.ds(lo + r0, chunk)] = first

    pieces = range(len(starts))

    def start_edges(s, par, pieced=False):
        if pieced:
            for q in pieces:
                each(zsides, lambda side: vq_copy(side, q).start())
        else:
            each(zsides, lambda side: vz_copy(side, s, par).start())
        each(ysides, lambda side: [vy_copy(side, s, group, par).start() for group in (0, 1)])

    def start_inner(s, par):
        if planes > 2:
            each(ysides, lambda side: vy_copy(side, s, 2, par).start())

    def setup_plane(p):
        act = [active[s][p - 1 : p + 2] for s in range(sections)]
        for r0 in starts:
            setup_chunk(p, r0, act)

    setup_plane(1)
    setup_plane(planes)
    for s in range(sections):
        start_edges(s, 1)
    for p in range(2, planes):
        setup_plane(p)
    for s in range(sections):
        start_inner(s, 1)

    table = factors()

    def relax_plane(s, p, now, new, alpha, beta):
        for r0 in starts:
            at = pl.ds(r0, chunk)
            mid = pl.ds(lo + r0, chunk)
            vs = [now[s, p, h, mid] for h in halves]
            vl, vr = left(vs), right(vs)
            for h in halves:
                v = vs[h]
                total = cxl[p - 1, h, at] * vl[h] + cxr[p - 1, h, at] * vr[h]
                total += cyu[p - 1, h, at] * now[s, p, h, pl.ds(lo + r0 - 1, chunk)]
                total += cyd[p - 1, h, at] * now[s, p, h, pl.ds(lo + r0 + 1, chunk)]
                total += cz[p - 1, h, at] * now[s, p - 1, h, mid]
                total += cz[p, h, at] * now[s, p + 1, h, mid]
                u = alpha * update[s, p - 1, h, at] + beta * (
                    (grad[s, p - 1, h, at] - v) + inverse[s, p - 1, h, at] * total
                )
                update[s, p - 1, h, at] = u
                new[s, p, h, mid] = v + u

    for n in range(2, SWEEPS + 1):
        now, new = (n - 1) % 2, n % 2
        for s in range(sections):
            relax = functools.partial(
                relax_plane, now=fields[now], new=fields[new], alpha=table[n - 2][0], beta=table[n - 2][1]
            )
            each(zsides, lambda side: vz_copy(1 - side, s, now).wait_recv())
            each(ysides, lambda side: [vy_copy(1 - side, s, group, now).wait_recv() for group in (0, 1)])

            def edge(i, _):
                relax(s, 1 + i * (planes - 1))
                return 0

            lax.fori_loop(0, 2, edge, 0)
            start_edges(s, new, n == SWEEPS and s == sections - 1)
            if planes > 2:
                each(ysides, lambda side: vy_copy(1 - side, s, 2, now).wait_recv())

                def inner(p, _):
                    relax(s, p)
                    return 0

                lax.fori_loop(2, planes, inner, 0)
                start_inner(s, new)
                each(ysides, lambda side: vy_copy(side, s, 2, now).wait_send())
            each(zsides, lambda side: vz_copy(side, s, now).wait_send())
            each(ysides, lambda side: [vy_copy(side, s, group, now).wait_send() for group in (0, 1)])

    last = SWEEPS % 2
    stores = [
        pltpu.make_async_copy(
            fields[last].at[:, pl.ds(1, planes), h, body],
            adj_ref.at[:, :, :, pl.ds(h * lanes, lanes)], store_sem.at[h],
        )
        for h in halves
    ]
    for store in stores:
        store.start()

    def ex_copy(k, p, slot):
        return remote(
            part_out.at[slot[0], p - 1], part_in.at[slot[1], p - 1], ex_send.at[k, p - 1],
            ex_recv.at[slot[1], p - 1], {"section": xpeer(k)},
        )

    def eq_copy(k, p, q, slot):
        edge, at = 0 if p == 1 else 1, pl.ds(starts[q], chunk)
        return remote(
            part_out.at[slot[0], p - 1, at], part_in.at[slot[1], p - 1, at], eq_send.at[k, edge, q],
            eq_recv.at[slot[1], edge, q], {"section": xpeer(k)},
        )

    def split_columns(totals):
        if width == lanes:
            return totals
        total = jnp.concatenate(totals, axis=-1)
        return [total[:, k * width : (k + 1) * width] for k in range(nx)]

    def energy_outer(p, q, outer):
        r0 = starts[q]
        at = pl.ds(lo + r0, chunk)
        totals = [0.0] * parts
        for s in range(sections):
            weight = 0.5 * active[s][p] * active[s][outer]
            for h in halves:
                dv = fields[last][s, p, h, at] - fields[last][s, outer, h, at]
                totals[h] += weight * (dv * (temp[s, p, h, at] - temp[s, outer, h, at]))
        for k, total in enumerate(split_columns(totals)):
            part_out[k, p - 1, pl.ds(r0, chunk)] += total
        for k in range(1, nx):
            eq_copy(k, p, q, (xpeer(k), me_x)).start()

    def energy_plane(p):
        for r0 in starts:
            rest = [0.0] * parts
            across = [0.0] * parts
            for s in range(sections):
                above, here, below = active[s][p - 1 : p + 2]

                def both(plane, h, shift):
                    at = pl.ds(lo + r0 + shift, chunk)
                    return fields[last][s, plane, h, at], temp[s, plane, h, at]

                pairs = [both(p, h, 0) for h in halves]
                vl, tl = left([v for v, _ in pairs]), left([t for _, t in pairs])
                for h in halves:
                    v, t = pairs[h]
                    across[h] += here * ((v - vl[h]) * (t - tl[h]))
                    v2, t2 = both(p, h, -1)
                    term = (v - v2) * (t - t2)
                    if r0 == 0:
                        term = term * up_mask
                    v2, t2 = both(p, h, 1)
                    more = (v - v2) * (t - t2)
                    if r0 == rows - chunk:
                        more = more * down_mask
                    term += more
                    if p > 1:
                        v2, t2 = both(p - 1, h, 0)
                        term += above * ((v - v2) * (t - t2))
                    if p < planes:
                        v2, t2 = both(p + 1, h, 0)
                        term += below * ((v - v2) * (t - t2))
                    rest[h] += here * term
            across[0] = jnp.where(lane == 0, 0.0, across[0])
            beyond = right(across)
            beyond[-1] = jnp.where(lane == lanes - 1, 0.0, beyond[-1])
            totals = [0.5 * (rest[h] + (across[h] + beyond[h])) for h in halves]
            for k, total in enumerate(split_columns(totals)):
                part_out[k, p - 1, pl.ds(r0, chunk)] = total
        for k in range(1, nx if 1 < p < planes else 1):
            ex_copy(k, p, (xpeer(k), me_x)).start()

    each(ysides, lambda side: ty_copy(1 - side).wait_recv())
    for s in range(sections):
        each(ysides, lambda side: [vy_copy(1 - side, s, g, last).wait_recv() for g in (0, 1)])
        if planes > 2:
            each(ysides, lambda side: vy_copy(1 - side, s, 2, last).wait_recv())
    for p in list(range(2, planes)) + [1, planes]:
        energy_plane(p)

    def finish(p, r0, number):
        at = pl.ds(r0, number)
        total = part_out[me_x, p - 1, at]
        for k in range(1, nx):
            total += part_in[xpeer(k), p - 1, at]
        m = share[me_x, p, pl.ds(lo + r0, number)]
        sens_ref[p - 1, at] = (-(1.0 - FLOOR_COND) * SIMP_POWER) * (m * m) * total

    for p in range(2, planes):
        for k in range(1, nx):
            ex_copy(k, p, (xpeer(k), xpeer(k))).wait_recv()
        for r0 in starts:
            finish(p, r0, chunk)

    each(zsides, lambda side: tz_copy(1 - side).wait_recv())
    for s in range(sections - 1):
        each(zsides, lambda side: vz_copy(1 - side, s, last).wait_recv())
    for q in pieces:
        each(zsides, lambda side: vq_copy(1 - side, q).wait_recv())
        energy_outer(1, q, 0)
        energy_outer(planes, q, planes + 1)

    for q in pieces:
        for p in (1, planes):
            for k in range(1, nx):
                eq_copy(k, p, q, (xpeer(k), xpeer(k))).wait_recv()
            finish(p, starts[q], chunk)

    for k in range(1, nx):
        mx_copy(k, me_x).wait_send()
        for p in range(2, planes):
            ex_copy(k, p, (xpeer(k), me_x)).wait_send()
        for q in pieces:
            for p in (1, planes):
                eq_copy(k, p, q, (xpeer(k), me_x)).wait_send()
    each(ysides, lambda side: [my_copy(side, k, me_x).wait_send() for k in range(nx)])
    each(zsides, lambda side: [mz_copy(side, k, me_x).wait_send() for k in range(nx)])
    each(ysides, lambda side: ty_copy(side).wait_send())
    each(zsides, lambda side: tz_copy(side).wait_send())
    for s in range(sections):
        if s < sections - 1:
            each(zsides, lambda side: vz_copy(side, s, last).wait_send())
        else:
            for q in pieces:
                each(zsides, lambda side: vq_copy(side, q).wait_send())
        each(ysides, lambda side: [vy_copy(side, s, g, last).wait_send() for g in (0, 1)])
        if planes > 2:
            each(ysides, lambda side: vy_copy(side, s, 2, last).wait_send())
    for store in stores:
        store.wait()


def solution(mesh):
    nz, nx, ny = mesh.shape["slab"], mesh.shape["section"], mesh.shape["col"]

    def body(material_share, stored_thermal_state, objective_slope, print_depths, slice_to_deposit):
        sections, planes, rows, cols = stored_thermal_state.shape
        width = material_share.shape[2]
        f32 = jnp.float32
        tall = rows + 2 * PAD
        dma = pltpu.SemaphoreType.DMA
        lanes = 128 if cols % 128 == 0 else cols
        split = cols // lanes
        steps = rows // min(32, rows)
        inner = (planes, split, rows, lanes)
        anywhere = pl.BlockSpec(memory_space=pltpu.HBM)
        return pl.pallas_call(
            functools.partial(kernel, (nz, nx, ny, slice_to_deposit.shape[0])),
            out_shape=(
                jax.ShapeDtypeStruct(stored_thermal_state.shape, f32),
                jax.ShapeDtypeStruct(material_share.shape, f32),
            ),
            in_specs=[anywhere] * 3 + [pl.BlockSpec(memory_space=pltpu.SMEM)] * 2,
            out_specs=(anywhere, pl.BlockSpec(memory_space=pltpu.VMEM)),
            scratch_shapes=[
                pltpu.VMEM((sections, planes + 2, split, tall, lanes), f32),
                pltpu.VMEM((sections, planes + 2, split, tall, lanes), f32),
                pltpu.VMEM((sections, planes + 2, split, tall, lanes), f32),
                pltpu.VMEM((sections,) + inner, f32),
                pltpu.VMEM((sections,) + inner, f32),
                pltpu.VMEM((sections,) + inner, f32),
                pltpu.VMEM((planes + 2, split, tall, lanes), f32),
                pltpu.VMEM((nx, planes + 2, tall, width), f32),
                pltpu.VMEM(inner, f32),
                pltpu.VMEM(inner, f32),
                pltpu.VMEM(inner, f32),
                pltpu.VMEM(inner, f32),
                pltpu.VMEM((planes + 1, split, rows, lanes), f32),
                pltpu.VMEM((nx, planes, rows, width), f32),
                pltpu.VMEM((nx, planes, rows, width), f32),
                dma((1 + 2 * split,)),
                dma((split,)),
                dma((nx,)), dma((nx,)),
                dma((2, nx)), dma((2, nx)),
                dma((2, nx)), dma((2, nx)),
                dma((2,)), dma((2,)),
                dma((2,)), dma((2,)),
                dma((2, sections, 2)), dma((2, sections, 2)),
                dma((2, sections, 3, 2)), dma((2, sections, 3, 2)),
                dma((nx, planes)), dma((nx, planes)),
                dma((nx, 2, steps)), dma((nx, 2, steps)),
                dma((2, steps)), dma((2, steps)),
            ],
            compiler_params=pltpu.CompilerParams(
                collective_id=0, has_side_effects=True, vmem_limit_bytes=63 * 1024 * 1024
            ),
        )(material_share, stored_thermal_state, objective_slope, print_depths, slice_to_deposit)

    return jax.shard_map(
        body,
        mesh=mesh,
        in_specs=(
            P(("parts", "slab"), "col", "section"),
            P(("parts", "section"), "slab", "col", None),
            P(("parts", "section"), "slab", "col", None),
            P(("parts", "section")),
            P("parts"),
        ),
        out_specs=(
            P(("parts", "section"), "slab", "col", None),
            P(("parts", "slab"), "col", "section"),
        ),
        check_vma=False,
    )
```
